32 devices in a mesh: seg: 2 (over y), tm: 4 (over x, core), state: 4 (over z).
Axes of the slice: x: 2, y: 2, z: 4, core: 2. Of those that a mesh axis runs over, the one named last changes fastest.
Arguments:
- observations: float32 [256, 512], P(('seg', 'tm')), parts along dimension 0, may hold values from -18 to 18
- gains: float32 [256, 512], P(('seg', 'tm')), parts along dimension 0, may hold values from 0.00078125 to 0.046875
- observed: int32 [256, 512], P(('seg', 'tm')), parts along dimension 0, may hold values 0 or 1
- pattern: int32 [8, 8], replicated, may hold values 0 or 1
- transition: float32 [512, 512], replicated, may hold values from -1 to 1
- initial_mean: float32 [1024], P('seg'), parts along dimension 0, may hold values from -6 to 6
Outputs:
- means: float32 [256, 512], P(('seg', 'tm'), 'state'), parts along dimension 0
The draws below stay inside these ranges and needn't reach their ends.
There are 2 independent parts, one for each index of `seg`. The reference program is written for one: setup_inputs(seed, part) draws one part's arguments, and reference() takes and returns one part's arrays. A program takes and returns all parts, laid end to end along the dimension named above; an argument that names none is the same for every part. Nothing has to cross between parts.
Inputs may be any that keep to these rules, and one draw needn't show every extreme that they name: Diagonal blocks count as present whatever pattern holds there.
All inputs are finite; a program needn't handle non-finite values. No bound on the sum of `observed` on one device may be relied on, other than what follows from the above.
Results may differ from the reference program's by a relative error of at most 0.0003.
Values sent between devices are 32-bit elements; how exact they have to be, the bound alone decides.
A program may use at most 128 MiB of HBM per device.

```python
import math
import jax
import jax.numpy as jnp
from jax import lax

D = 512
NB = 8
FRAMES = 128


def set_ends(values, rng, smallest, largest):
    place = [jax.random.randint(jax.random.fold_in(rng, axis), (), 0, length) for axis, length in enumerate(values.shape)]
    longest = values.shape.index(max(values.shape))
    next_to = place[:longest] + [(place[longest] + 1) % values.shape[longest]] + place[longest + 1:]
    return values.at[tuple(place)].set(smallest).at[tuple(next_to)].set(largest)


def levels(rng, dims, shards, low, high):
    loudness, own = 1.0, jax.random.fold_in(rng, 6)
    for position, shards_of in shards:
        heights = jnp.exp(jax.random.uniform(jax.random.fold_in(own, position), (shards_of,), jnp.float32, low / len(shards), high / len(shards)))
        loudness = loudness * jnp.repeat(heights, dims[position] // shards_of).reshape([-1 if axis == position else 1 for axis in range(len(dims))])
    return loudness


def gaussian(key, extent, width, reach, cuts=(), held_as=jnp.bfloat16):
    array = width * jax.random.normal(key, extent, jnp.float32)
    if cuts:
        array = array * levels(key, extent, cuts, -0.22, 0.18)
    return jnp.clip(array, -reach, reach).astype(held_as)


def setup_inputs(seed: int = 0, part: int = 0) -> dict:
    keys = jax.random.split(jax.random.key(seed), 7)
    part_splits = jax.random.split(jax.random.fold_in(keys[6], part), 7)
    observations = gaussian(part_splits[0], (FRAMES, D), 3.0, 18.0, ((0, 4),), jnp.float32)
    gains = jnp.clip(jnp.exp(math.log(0.046875) - 4.0943445 * jax.random.uniform(part_splits[1], (FRAMES, D), jnp.float32) ** levels(part_splits[1], (FRAMES, D), ((0, 4),), -0.2, 0.2)), 0.00078125, 0.046875)
    observed = set_ends((jax.random.randint(part_splits[2], (FRAMES, D), 0, 3) < 1).astype(jnp.int32), jax.random.fold_in(part_splits[2], 1), 0, 1)
    pattern = set_ends((jax.random.randint(keys[3], (NB, NB), 0, 2) < 1).astype(jnp.int32), jax.random.fold_in(keys[3], 1), 0, 1)
    transition = gaussian(keys[4], (D, D), (D // 16) ** -0.5, 1.0, (), jnp.float32)
    initial_mean = gaussian(part_splits[5], (D,), 1.0, 6.0, (), jnp.float32)
    return {"observations": observations, "gains": gains, "observed": observed, "pattern": pattern, "transition": transition, "initial_mean": initial_mean}


def build_transition(pattern, transition):
    blocks = pattern.shape[0]
    size = transition.shape[0]
    block = size // blocks
    present = jnp.maximum(pattern, jnp.eye(blocks, dtype=jnp.int32)).astype(jnp.float32)
    expand = jnp.repeat(jnp.repeat(present, block, axis=0), block, axis=1)
    masked = transition * expand
    skew = 0.5 * (masked - masked.T)
    eye = jnp.eye(size, dtype=jnp.float32)
    plus = eye + skew
    normal = eye + jnp.dot(skew.T, skew, precision=lax.Precision.HIGHEST)
    factor = jnp.linalg.cholesky(normal)
    solved = jax.scipy.linalg.cho_solve((factor, True), plus)
    return jnp.dot(plus, solved, precision=lax.Precision.HIGHEST)

def reference(observations, gains, observed, pattern, transition, initial_mean):
    full = build_transition(pattern, transition)
    seen = observed.astype(jnp.float32)
    damp = 1.0 - gains * seen
    drive = gains * seen * observations

    def step(mean, inputs):
        damp_row, drive_row = inputs
        nxt = damp_row * jnp.dot(full, mean, precision=lax.Precision.HIGHEST) + drive_row
        return (nxt, nxt)
    final, means = lax.scan(step, initial_mean.astype(jnp.float32), (damp, drive))
    return means
```

```python
import functools

import jax
import jax.numpy as jnp
from jax import lax
from jax.experimental import pallas as pl
from jax.experimental.pallas import tpu as pltpu
from jax.sharding import PartitionSpec as P

F32 = jnp.float32
BF16 = jnp.bfloat16
VMEM = pl.BlockSpec(memory_space=pltpu.VMEM)


def split(a):
    high = a.astype(BF16)
    return high, (a - high.astype(F32)).astype(BF16)


def dot1(a, b):
    return jnp.dot(a, b, preferred_element_type=F32)


def eye_of(size):
    rows = lax.broadcasted_iota(jnp.int32, (size, size), 0)
    cols = lax.broadcasted_iota(jnp.int32, (size, size), 1)
    return (rows == cols).astype(F32)


def total(a):
    return jnp.sum(jnp.sum(a, axis=0, keepdims=True), axis=1, keepdims=True)


def build_kernel(pattern_ref, transition_ref, ft_ref, s_hi, s_lo, n_hi, x_ref, y_ref, r_ref, y_hi, y_lo):
    size = transition_ref.shape[0]
    blocks = pattern_ref.shape[0]
    block = size // blocks
    eye = functools.partial(eye_of, size)

    tall = (
        lax.broadcasted_iota(jnp.int32, (size, blocks), 0) // block
        == lax.broadcasted_iota(jnp.int32, (size, blocks), 1)
    ).astype(BF16)
    wide = (
        lax.broadcasted_iota(jnp.int32, (blocks, size), 1) // block
        == lax.broadcasted_iota(jnp.int32, (blocks, size), 0)
    ).astype(BF16)
    present = jnp.maximum(pattern_ref[...].astype(F32), eye_of(blocks)).astype(BF16)
    expand = dot1(dot1(tall, present).astype(BF16), wide)
    masked = transition_ref[...] * expand
    skew = 0.5 * (masked.T - masked)
    high, low = split(skew)
    s_hi[...] = high
    s_lo[...] = low

    normal = eye() - dot1(high, high)
    n_hi[...] = normal.astype(BF16)
    square = dot1(n_hi[...], n_hi[...])
    bound = 1.02 * jnp.sqrt(jnp.sqrt(0.5 * total(square * square)))
    bound = jnp.maximum(bound, 1.0001)

    def rescale(rho):
        worst = jnp.minimum(rho * rho, 1.0)
        return 2.0 / (2.0 - worst), worst / (2.0 - worst)

    alpha = 2.0 / (1.0 + bound)
    factor, rho = rescale((bound - 1.0) / (bound + 1.0))
    x_ref[...] = (factor * alpha) * (2.0 * eye() - alpha * normal)

    def more(carry):
        step, rho = carry
        return jnp.logical_and(jnp.max(rho) > 0.03, step < 24)

    def newton(carry):
        step, rho = carry
        x_hi = x_ref[...].astype(BF16)
        res = eye() - dot1(n_hi[...], x_hi)
        factor, rho = rescale(rho)
        x_ref[...] = factor * (x_ref[...] + dot1(x_hi, res.astype(BF16)))
        return step + 1, rho

    lax.while_loop(more, newton, (0, rho))
    y_ref[...] = x_ref[...] + dot1(x_ref[...].astype(BF16), s_hi[...])

    def residual():
        high, low = split(y_ref[...])
        y_hi[...] = high
        y_lo[...] = low
        prod = dot1(s_hi[...], y_lo[...]) + dot1(s_lo[...], y_hi[...])
        res = eye() - y_ref[...] + (prod + dot1(s_hi[...], y_hi[...]))
        r_ref[...] = res
        return jnp.max(total(res * res))

    first = residual()
    good = first < 0.5

    @pl.when(jnp.logical_not(good))
    def _():
        y_ref[...] = (1.9 / (1.0 + bound)) * (
            eye() + (s_hi[...].astype(F32) + s_lo[...].astype(F32))
        )
        residual()

    def unfinished(carry):
        step, size2 = carry
        return jnp.logical_and(jnp.logical_not(size2 < 6e-5), step < 64)

    def refine(carry):
        step, unused = carry
        r_hi, r_lo = split(r_ref[...])
        prod = dot1(y_hi[...], r_lo) + dot1(y_lo[...], r_hi)
        y_ref[...] += prod + dot1(y_hi[...], r_hi)
        return step + 1, residual()

    lax.while_loop(unfinished, refine, (0, jnp.where(good, first, 1e9)))
    last = y_ref[...] + dot1(y_hi[...], r_ref[...].astype(BF16))
    ft_ref[...] = 2.0 * last - eye()


def build(pattern, transition):
    size = transition.shape[0]
    square = (size, size)
    return pl.pallas_call(
        build_kernel,
        out_shape=jax.ShapeDtypeStruct(square, F32),
        in_specs=[VMEM, VMEM],
        out_specs=VMEM,
        scratch_shapes=[
            pltpu.VMEM(square, BF16),
            pltpu.VMEM(square, BF16),
            pltpu.VMEM(square, BF16),
            pltpu.VMEM(square, F32),
            pltpu.VMEM(square, F32),
            pltpu.VMEM(square, F32),
            pltpu.VMEM(square, BF16),
            pltpu.VMEM(square, BF16),
        ],
        compiler_params=pltpu.CompilerParams(vmem_limit_bytes=40 << 20),
        cost_estimate=pl.CostEstimate(
            flops=40 * size**3, bytes_accessed=8 * size**2, transcendentals=0
        ),
        name="build_transition",
    )(pattern, transition)


def scan_kernel(ft_ref, frames_ref, start_ref, out_ref, kept):
    size = ft_ref.shape[0]
    frames, width = out_ref.shape
    mine = lax.axis_index("tm")
    offset = 0 if width == size else lax.axis_index("state") * width

    def step(t, row):
        acc = [jnp.zeros((8, size), F32), jnp.zeros((8, size), F32)]
        for tile in range(size // 128):
            piece = row[:, 128 * tile : 128 * tile + 128]
            column = jnp.broadcast_to(piece, (128, 128)).T
            for group in range(16):
                at = 128 * tile + 8 * group
                spread = jnp.concatenate([column[8 * group : 8 * group + 8]] * (size // 128), 1)
                acc[group % 2] += ft_ref[at : at + 8, :] * spread
        moved = jnp.sum(acc[0] + acc[1], axis=0, keepdims=True)
        damp = frames_ref[pl.ds(t, 1), pl.ds(0, size)]
        drive = frames_ref[pl.ds(t, 1), pl.ds(size, size)]
        row = damp * moved + drive
        kept[pl.ds(t, 1), :] = row
        return row

    lax.fori_loop(0, (mine + 1) * frames, step, start_ref[...])
    out_ref[...] = kept[
        pl.ds(pl.multiple_of(mine * frames, frames), frames),
        pl.ds(0, size) if width == size else pl.ds(pl.multiple_of(offset, width), width),
    ]


def body(observations, gains, observed, pattern, transition, initial_mean):
    frames, size = observations.shape
    width = size // lax.axis_size("state")
    seen = gains * observed.astype(F32)
    packed = jnp.concatenate([1.0 - seen, seen * observations], axis=1)
    packed = lax.all_gather(packed, "tm", axis=0, tiled=True)
    ft = build(pattern, transition)
    kept_width = width if width % 128 == 0 else size
    means = pl.pallas_call(
        scan_kernel,
        out_shape=jax.ShapeDtypeStruct((frames, kept_width), F32),
        in_specs=[VMEM, VMEM, VMEM],
        out_specs=VMEM,
        scratch_shapes=[pltpu.VMEM((packed.shape[0], size), F32)],
        compiler_params=pltpu.CompilerParams(vmem_limit_bytes=40 << 20),
        name="scan_frames",
    )(ft, packed, initial_mean.reshape(1, size))
    if kept_width == width:
        return means
    return lax.dynamic_slice_in_dim(means, lax.axis_index("state") * width, width, 1)


def solution(mesh):
    return jax.shard_map(
        body,
        mesh=mesh,
        in_specs=(
            P(("seg", "tm"), None),
            P(("seg", "tm"), None),
            P(("seg", "tm"), None),
            P(),
            P(),
            P("seg"),
        ),
        out_specs=P(("seg", "tm"), "state"),
        check_vma=False,
    )
```

```python
import functools

import jax
import jax.numpy as jnp
from jax import lax
from jax.experimental import pallas as pl
from jax.experimental.pallas import tpu as pltpu
from jax.sharding import PartitionSpec as P

F32 = jnp.float32
BF16 = jnp.bfloat16
VMEM = pl.BlockSpec(memory_space=pltpu.VMEM)
MESH = pl.DeviceIdType.MESH
NEWTON_STEPS = 3


def split(a):
    high = a.astype(BF16)
    return high, (a - high.astype(F32)).astype(BF16)


def dot1(a, b):
    return jnp.dot(a, b, preferred_element_type=F32)


def eye_of(size):
    rows = lax.broadcasted_iota(jnp.int32, (size, size), 0)
    cols = lax.broadcasted_iota(jnp.int32, (size, size), 1)
    return (rows == cols).astype(F32)


def total(a):
    return jnp.sum(jnp.sum(a, axis=0, keepdims=True), axis=1, keepdims=True)


def share_and_build_kernel(
    observations_ref, gains_ref, observed_ref, pattern_ref, transition_ref,
    y_ref, s_hi, s_lo, packed_ref,
    own, slots, n_hi, x_ref, send_sem, recv_sem,
):
    size = transition_ref.shape[0]
    blocks = pattern_ref.shape[0]
    block = size // blocks
    frames = observations_ref.shape[0]
    count = slots.shape[0]
    mine = lax.axis_index("tm")
    eye = functools.partial(eye_of, size)

    barrier = pltpu.get_barrier_semaphore()
    for hop in range(1, count):
        pl.semaphore_signal(
            barrier, inc=1, device_id={"tm": lax.rem(mine + hop, count)}, device_id_type=MESH
        )
    seen = gains_ref[...] * observed_ref[...].astype(F32)
    own[:, :size] = 1.0 - seen
    own[:, size:] = seen * observations_ref[...]
    pl.semaphore_wait(barrier, count - 1)
    copies = []
    for hop in range(1, count):
        copy = pltpu.make_async_remote_copy(
            src_ref=own,
            dst_ref=slots.at[mine],
            send_sem=send_sem.at[hop],
            recv_sem=recv_sem.at[hop],
            device_id={"tm": lax.rem(mine + hop, count)},
            device_id_type=MESH,
        )
        copy.start()
        copies.append(copy)

    tall = (
        lax.broadcasted_iota(jnp.int32, (size, blocks), 0) // block
        == lax.broadcasted_iota(jnp.int32, (size, blocks), 1)
    ).astype(BF16)
    wide = (
        lax.broadcasted_iota(jnp.int32, (blocks, size), 1) // block
        == lax.broadcasted_iota(jnp.int32, (blocks, size), 0)
    ).astype(BF16)
    present = jnp.maximum(pattern_ref[...].astype(F32), eye_of(blocks)).astype(BF16)
    expand = dot1(dot1(tall, present).astype(BF16), wide)
    masked = transition_ref[...] * expand
    skew = 0.5 * (masked.T - masked)
    high, low = split(skew)
    s_hi[...] = high
    s_lo[...] = low

    normal = eye() - dot1(high, high)
    n_hi[...] = normal.astype(BF16)
    square = dot1(n_hi[...], n_hi[...])
    bound = 1.02 * jnp.sqrt(jnp.sqrt(0.5 * total(square * square)))
    bound = jnp.maximum(bound, 1.0001)

    def rescale(rho):
        worst = jnp.minimum(rho * rho, 1.0)
        return 2.0 / (2.0 - worst), worst / (2.0 - worst)

    alpha = 2.0 / (1.0 + bound)
    factor, rho = rescale((bound - 1.0) / (bound + 1.0))
    x_ref[...] = (factor * alpha) * (2.0 * eye() - alpha * normal)

    def newton(step, rho):
        x_hi = x_ref[...].astype(BF16)
        res = eye() - dot1(n_hi[...], x_hi)
        factor, rho = rescale(rho)
        x_ref[...] = factor * (x_ref[...] + dot1(x_hi, res.astype(BF16)))
        return rho

    lax.fori_loop(0, NEWTON_STEPS, newton, rho)
    y_ref[...] = x_ref[...] + dot1(x_ref[...].astype(BF16), s_hi[...])

    for copy in copies:
        copy.wait_recv()
    for place in range(count):
        rows = pl.ds(place * frames, frames)

        @pl.when(mine == place)
        def _():
            packed_ref[rows, :] = own[...]

        @pl.when(mine != place)
        def _():
            packed_ref[rows, :] = slots[place]

    for copy in copies:
        copy.wait_send()


def share_and_build(observations, gains, observed, pattern, transition):
    frames, size = observations.shape
    count = lax.axis_size("tm")
    square = (size, size)
    return pl.pallas_call(
        share_and_build_kernel,
        out_shape=(
            jax.ShapeDtypeStruct(square, F32),
            jax.ShapeDtypeStruct(square, BF16),
            jax.ShapeDtypeStruct(square, BF16),
            jax.ShapeDtypeStruct((count * frames, 2 * size), F32),
        ),
        in_specs=[VMEM] * 5,
        out_specs=(VMEM,) * 4,
        scratch_shapes=[
            pltpu.VMEM((frames, 2 * size), F32),
            pltpu.VMEM((count, frames, 2 * size), F32),
            pltpu.VMEM(square, BF16),
            pltpu.VMEM(square, F32),
            pltpu.SemaphoreType.DMA((count,)),
            pltpu.SemaphoreType.DMA((count,)),
        ],
        compiler_params=pltpu.CompilerParams(
            vmem_limit_bytes=40 << 20, collective_id=0, has_side_effects=True
        ),
        name="share_and_build",
    )(observations, gains, observed, pattern, transition)


def refine_to_transition(y_ref, s_hi, s_lo, ft_ref, r_ref, y_hi, y_lo):
    size = y_ref.shape[0]
    eye = functools.partial(eye_of, size)

    def residual():
        high, low = split(ft_ref[...])
        y_hi[...] = high
        y_lo[...] = low
        prod = dot1(s_hi[...], y_lo[...]) + dot1(s_lo[...], y_hi[...])
        res = eye() - ft_ref[...] + (prod + dot1(s_hi[...], y_hi[...]))
        r_ref[...] = res
        return jnp.max(total(res * res))

    ft_ref[...] = y_ref[...]
    first = residual()
    good = first < 0.5

    @pl.when(jnp.logical_not(good))
    def _():
        skew = s_hi[...].astype(F32) + s_lo[...].astype(F32)
        ft_ref[...] = (1.9 / (2.0 + total(skew * skew))) * (eye() + skew)
        residual()

    def unfinished(carry):
        step, size2 = carry
        return jnp.logical_and(jnp.logical_not(size2 < 6e-5), step < 64)

    def refine(carry):
        step, unused = carry
        r_hi, r_lo = split(r_ref[...])
        prod = dot1(y_hi[...], r_lo) + dot1(y_lo[...], r_hi)
        ft_ref[...] += prod + dot1(y_hi[...], r_hi)
        return step + 1, residual()

    lax.while_loop(unfinished, refine, (0, jnp.where(good, first, 1e9)))
    last = ft_ref[...] + dot1(y_hi[...], r_ref[...].astype(BF16))
    ft_ref[...] = 2.0 * last - eye()


def scan_kernel(y_ref, s_hi, s_lo, frames_ref, start_ref, out_ref, ft_ref, r_ref, y_hi, y_lo, kept):
    refine_to_transition(y_ref, s_hi, s_lo, ft_ref, r_ref, y_hi, y_lo)
    size = ft_ref.shape[0]
    frames, width = out_ref.shape
    mine = lax.axis_index("tm")
    offset = 0 if width == size else lax.axis_index("state") * width

    def step(t, row):
        acc = [jnp.zeros((8, size), F32), jnp.zeros((8, size), F32)]
        for tile in range(size // 128):
            piece = row[:, 128 * tile : 128 * tile + 128]
            column = jnp.broadcast_to(piece, (128, 128)).T
            for group in range(16):
                at = 128 * tile + 8 * group
                spread = jnp.concatenate([column[8 * group : 8 * group + 8]] * (size // 128), 1)
                acc[group % 2] += ft_ref[at : at + 8, :] * spread
        moved = jnp.sum(acc[0] + acc[1], axis=0, keepdims=True)
        damp = frames_ref[pl.ds(t, 1), pl.ds(0, size)]
        drive = frames_ref[pl.ds(t, 1), pl.ds(size, size)]
        row = damp * moved + drive
        kept[pl.ds(t, 1), :] = row
        return row

    lax.fori_loop(0, (mine + 1) * frames, step, start_ref[...])
    out_ref[...] = kept[
        pl.ds(pl.multiple_of(mine * frames, frames), frames),
        pl.ds(0, size) if width == size else pl.ds(pl.multiple_of(offset, width), width),
    ]


def body(observations, gains, observed, pattern, transition, initial_mean):
    frames, size = observations.shape
    width = size // lax.axis_size("state")
    start, s_hi, s_lo, packed = share_and_build(
        observations, gains, observed, pattern, transition
    )
    kept_width = width if width % 128 == 0 else size
    square = (size, size)
    means = pl.pallas_call(
        scan_kernel,
        out_shape=jax.ShapeDtypeStruct((frames, kept_width), F32),
        in_specs=[VMEM] * 5,
        out_specs=VMEM,
        scratch_shapes=[
            pltpu.VMEM(square, F32),
            pltpu.VMEM(square, F32),
            pltpu.VMEM(square, BF16),
            pltpu.VMEM(square, BF16),
            pltpu.VMEM((packed.shape[0], size), F32),
        ],
        compiler_params=pltpu.CompilerParams(vmem_limit_bytes=40 << 20),
        name="refine_and_scan",
    )(start, s_hi, s_lo, packed, initial_mean.reshape(1, size))
    if kept_width == width:
        return means
    return lax.dynamic_slice_in_dim(means, lax.axis_index("state") * width, width, 1)


def solution(mesh):
    return jax.shard_map(
        body,
        mesh=mesh,
        in_specs=(
            P(("seg", "tm"), None),
            P(("seg", "tm"), None),
            P(("seg", "tm"), None),
            P(),
            P(),
            P("seg"),
        ),
        out_specs=P(("seg", "tm"), "state"),
        check_vma=False,
    )
```

```python
import functools

import jax
import jax.numpy as jnp
from jax import lax
from jax.experimental import pallas as pl
from jax.experimental.pallas import tpu as pltpu
from jax.sharding import PartitionSpec as P

F32 = jnp.float32
BF16 = jnp.bfloat16
VMEM = pl.BlockSpec(memory_space=pltpu.VMEM)
HBM = pl.BlockSpec(memory_space=pltpu.HBM)
MESH = pl.DeviceIdType.MESH
NEWTON_STEPS = 3


def split(a):
    high = a.astype(BF16)
    return high, (a - high.astype(F32)).astype(BF16)


def dot1(a, b):
    return jnp.dot(a, b, preferred_element_type=F32)


def eye_of(size):
    rows = lax.broadcasted_iota(jnp.int32, (size, size), 0)
    cols = lax.broadcasted_iota(jnp.int32, (size, size), 1)
    return (rows == cols).astype(F32)


def total(a):
    return jnp.sum(jnp.sum(a, axis=0, keepdims=True), axis=1, keepdims=True)


def share_and_build_kernel(
    observations_hbm, gains_hbm, observed_hbm, pattern_hbm, transition_hbm,
    y_hbm, s_hi_hbm, s_lo_hbm, packed_hbm,
    y_ref, s_hi, s_lo,
    observations_ref, gains_ref, observed_ref, pattern_ref, transition_ref,
    own, slots, n_hi, x_ref, load_sem, save_sem, send_sem, recv_sem,
):
    loads = []
    for place, (source, target) in enumerate((
        (observations_hbm, observations_ref),
        (gains_hbm, gains_ref),
        (observed_hbm, observed_ref),
        (pattern_hbm, pattern_ref),
        (transition_hbm, transition_ref),
    )):
        loads.append(pltpu.make_async_copy(source, target, load_sem.at[place]))
        loads[-1].start()
    size = transition_ref.shape[0]
    blocks = pattern_ref.shape[0]
    block = size // blocks
    frames = observations_ref.shape[0]
    count = slots.shape[0]
    mine = lax.axis_index("tm")
    eye = functools.partial(eye_of, size)

    chips = count // 2
    core = lax.rem(mine, 2)
    chip = mine // 2
    partner = {"tm": 2 * chip + 1 - core}
    others = [2 * lax.rem(chip + hop, chips) + core for hop in range(1, chips)]
    sources = [2 * lax.rem(chip + chips - hop, chips) + core for hop in range(1, chips)]

    barrier = pltpu.get_barrier_semaphore()
    for target in [partner] + [{"tm": other} for other in others]:
        pl.semaphore_signal(barrier, inc=1, device_id=target, device_id_type=MESH)
    for load in loads[:3]:
        load.wait()
    seen = gains_ref[...] * observed_ref[...].astype(F32)
    own[:, :size] = 1.0 - seen
    own[:, size:] = seen * observations_ref[...]
    pl.semaphore_wait(barrier, chips)

    def send(source, place, target, sem):
        copy = pltpu.make_async_remote_copy(
            src_ref=source,
            dst_ref=slots.at[place],
            send_sem=send_sem.at[sem],
            recv_sem=recv_sem.at[sem],
            device_id=target,
            device_id_type=MESH,
        )
        copy.start()
        return copy

    direct = [
        send(own, mine, {"tm": other}, hop) for hop, other in enumerate(others, 1)
    ]
    passed = [send(own, mine, partner, 0)]

    for load in loads[3:]:
        load.wait()
    tall = (
        lax.broadcasted_iota(jnp.int32, (size, blocks), 0) // block
        == lax.broadcasted_iota(jnp.int32, (size, blocks), 1)
    ).astype(BF16)
    wide = (
        lax.broadcasted_iota(jnp.int32, (blocks, size), 1) // block
        == lax.broadcasted_iota(jnp.int32, (blocks, size), 0)
    ).astype(BF16)
    present = jnp.maximum(pattern_ref[...].astype(F32), eye_of(blocks)).astype(BF16)
    expand = dot1(dot1(tall, present).astype(BF16), wide)
    masked = transition_ref[...] * expand
    skew = 0.5 * (masked.T - masked)
    high, low = split(skew)
    s_hi[...] = high
    s_lo[...] = low
    saves = [
        pltpu.make_async_copy(s_hi, s_hi_hbm, save_sem.at[0]),
        pltpu.make_async_copy(s_lo, s_lo_hbm, save_sem.at[1]),
    ]
    for save in saves:
        save.start()

    normal = eye() - dot1(high, high)
    n_hi[...] = normal.astype(BF16)
    square = dot1(n_hi[...], n_hi[...])
    bound = 1.02 * jnp.sqrt(jnp.sqrt(0.5 * total(square * square)))
    bound = jnp.maximum(bound, 1.0001)

    def rescale(rho):
        worst = jnp.minimum(rho * rho, 1.0)
        return 2.0 / (2.0 - worst), worst / (2.0 - worst)

    alpha = 2.0 / (1.0 + bound)
    factor, rho = rescale((bound - 1.0) / (bound + 1.0))
    x_ref[...] = (factor * alpha) * (2.0 * eye() - alpha * normal)

    def newton(step, rho):
        x_hi = x_ref[...].astype(BF16)
        res = eye() - dot1(n_hi[...], x_hi)
        factor, rho = rescale(rho)
        x_ref[...] = factor * (x_ref[...] + dot1(x_hi, res.astype(BF16)))
        return rho

    rho = lax.fori_loop(0, NEWTON_STEPS - 1, newton, rho)
    for hop, source in enumerate(sources, 1):
        direct[hop - 1].wait_recv()
        passed.append(send(slots.at[source], source, partner, chips + hop))
    newton(0, rho)
    y_ref[...] = x_ref[...] + dot1(x_ref[...].astype(BF16), s_hi[...])

    saves.append(pltpu.make_async_copy(y_ref, y_hbm, save_sem.at[2]))
    saves[-1].start()
    for copy in passed:
        copy.wait_recv()
    slots[mine] = own[...]
    saves.append(pltpu.make_async_copy(slots, packed_hbm, save_sem.at[3]))
    saves[-1].start()
    for save in saves:
        save.wait()
    for copy in direct + passed:
        copy.wait_send()


def share_and_build(observations, gains, observed, pattern, transition):
    frames, size = observations.shape
    count = lax.axis_size("tm")
    square = (size, size)
    return pl.pallas_call(
        share_and_build_kernel,
        out_shape=(
            jax.ShapeDtypeStruct(square, F32),
            jax.ShapeDtypeStruct(square, BF16),
            jax.ShapeDtypeStruct(square, BF16),
            jax.ShapeDtypeStruct((count, frames, 2 * size), F32),
        ),
        in_specs=[HBM] * 5,
        out_specs=(HBM,) * 4,
        scratch_shapes=[
            pltpu.VMEM(square, F32),
            pltpu.VMEM(square, BF16),
            pltpu.VMEM(square, BF16),
            pltpu.VMEM((frames, size), F32),
            pltpu.VMEM((frames, size), F32),
            pltpu.VMEM((frames, size), jnp.int32),
            pltpu.VMEM(pattern.shape, jnp.int32),
            pltpu.VMEM(square, F32),
            pltpu.VMEM((frames, 2 * size), F32),
            pltpu.VMEM((count, frames, 2 * size), F32),
            pltpu.VMEM(square, BF16),
            pltpu.VMEM(square, F32),
            pltpu.SemaphoreType.DMA((5,)),
            pltpu.SemaphoreType.DMA((4,)),
            pltpu.SemaphoreType.DMA((count,)),
            pltpu.SemaphoreType.DMA((count,)),
        ],
        compiler_params=pltpu.CompilerParams(
            vmem_limit_bytes=60 << 20, collective_id=0, has_side_effects=True
        ),
        name="share_and_build",
    )(observations, gains, observed, pattern, transition)


def refine_to_transition(s_hi, s_lo, ft_ref, r_ref, y_hi, y_lo):
    size = ft_ref.shape[0]
    eye = functools.partial(eye_of, size)

    def residual():
        high, low = split(ft_ref[...])
        y_hi[...] = high
        y_lo[...] = low
        prod = dot1(s_hi[...], y_lo[...]) + dot1(s_lo[...], y_hi[...])
        res = eye() - ft_ref[...] + (prod + dot1(s_hi[...], y_hi[...]))
        r_ref[...] = res
        return jnp.max(total(res * res))

    first = residual()
    good = first < 0.5

    @pl.when(jnp.logical_not(good))
    def _():
        skew = s_hi[...].astype(F32) + s_lo[...].astype(F32)
        ft_ref[...] = (1.9 / (2.0 + total(skew * skew))) * (eye() + skew)
        residual()

    def unfinished(carry):
        step, size2 = carry
        return jnp.logical_and(jnp.logical_not(size2 < 6e-5), step < 64)

    def refine(carry):
        step, unused = carry
        r_hi, r_lo = split(r_ref[...])
        prod = dot1(y_hi[...], r_lo) + dot1(y_lo[...], r_hi)
        ft_ref[...] += prod + dot1(y_hi[...], r_hi)
        return step + 1, residual()

    lax.while_loop(unfinished, refine, (0, jnp.where(good, first, 1e9)))
    last = ft_ref[...] + dot1(y_hi[...], r_ref[...].astype(BF16))
    ft_ref[...] = 2.0 * last - eye()


def scan_kernel(
    y_hbm, s_hi_hbm, s_lo_hbm, frames_hbm, start_hbm, out_ref,
    ft_ref, s_hi, s_lo, frames_ref, start_ref, r_ref, y_hi, y_lo, kept, load_sem,
):
    loads = []
    for place, (source, target) in enumerate((
        (y_hbm, ft_ref),
        (s_hi_hbm, s_hi),
        (s_lo_hbm, s_lo),
        (frames_hbm, frames_ref),
        (start_hbm, start_ref),
    )):
        loads.append(pltpu.make_async_copy(source, target, load_sem.at[place]))
        loads[-1].start()
    for load in loads[:3]:
        load.wait()
    refine_to_transition(s_hi, s_lo, ft_ref, r_ref, y_hi, y_lo)
    for load in loads[3:]:
        load.wait()
    size = ft_ref.shape[0]
    frames, width = out_ref.shape
    mine = lax.axis_index("tm")
    offset = 0 if width == size else lax.axis_index("state") * width

    def step(t, row):
        acc = [jnp.zeros((8, size), F32), jnp.zeros((8, size), F32)]
        for tile in range(size // 128):
            piece = row[:, 128 * tile : 128 * tile + 128]
            column = jnp.broadcast_to(piece, (128, 128)).T
            for group in range(16):
                at = 128 * tile + 8 * group
                spread = jnp.concatenate([column[8 * group : 8 * group + 8]] * (size // 128), 1)
                acc[group % 2] += ft_ref[at : at + 8, :] * spread
        moved = jnp.sum(acc[0] + acc[1], axis=0, keepdims=True)
        damp = frames_ref[pl.ds(t, 1), :size]
        drive = frames_ref[pl.ds(t, 1), size:]
        row = damp * moved + drive
        kept[pl.ds(t, 1), :] = row
        return row

    lax.fori_loop(0, (mine + 1) * frames, step, start_ref[...])
    out_ref[...] = kept[
        pl.ds(pl.multiple_of(mine * frames, frames), frames),
        pl.ds(0, size) if width == size else pl.ds(pl.multiple_of(offset, width), width),
    ]


def body(observations, gains, observed, pattern, transition, initial_mean):
    frames, size = observations.shape
    width = size // lax.axis_size("state")
    start, s_hi, s_lo, packed = share_and_build(
        observations, gains, observed, pattern, transition
    )
    packed = packed.reshape(-1, 2 * size)
    kept_width = width if width % 128 == 0 else size
    square = (size, size)
    means = pl.pallas_call(
        scan_kernel,
        out_shape=jax.ShapeDtypeStruct((frames, kept_width), F32),
        in_specs=[HBM] * 5,
        out_specs=VMEM,
        scratch_shapes=[
            pltpu.VMEM(square, F32),
            pltpu.VMEM(square, BF16),
            pltpu.VMEM(square, BF16),
            pltpu.VMEM((packed.shape[0], 2 * size), F32),
            pltpu.VMEM((1, size), F32),
            pltpu.VMEM(square, F32),
            pltpu.VMEM(square, BF16),
            pltpu.VMEM(square, BF16),
            pltpu.VMEM((packed.shape[0], size), F32),
            pltpu.SemaphoreType.DMA((5,)),
        ],
        compiler_params=pltpu.CompilerParams(vmem_limit_bytes=60 << 20),
        name="refine_and_scan",
    )(start, s_hi, s_lo, packed, initial_mean.reshape(1, size))
    if kept_width == width:
        return means
    return lax.dynamic_slice_in_dim(means, lax.axis_index("state") * width, width, 1)


def solution(mesh):
    return jax.shard_map(
        body,
        mesh=mesh,
        in_specs=(
            P(("seg", "tm"), None),
            P(("seg", "tm"), None),
            P(("seg", "tm"), None),
            P(),
            P(),
            P("seg"),
        ),
        out_specs=P(("seg", "tm"), "state"),
        check_vma=False,
    )
```

```python
import functools

import jax
import jax.numpy as jnp
from jax import lax
from jax.experimental import pallas as pl
from jax.experimental.pallas import tpu as pltpu
from jax.sharding import PartitionSpec as P

F32 = jnp.float32
BF16 = jnp.bfloat16
VMEM = pl.BlockSpec(memory_space=pltpu.VMEM)
HBM = pl.BlockSpec(memory_space=pltpu.HBM)
MESH = pl.DeviceIdType.MESH
NEWTON_STEPS = 3


def split(a):
    high = a.astype(BF16)
    return high, (a - high.astype(F32)).astype(BF16)


def dot1(a, b):
    return jnp.dot(a, b, preferred_element_type=F32)


def eye_of(size):
    rows = lax.broadcasted_iota(jnp.int32, (size, size), 0)
    cols = lax.broadcasted_iota(jnp.int32, (size, size), 1)
    return (rows == cols).astype(F32)


def total(a):
    return jnp.sum(jnp.sum(a, axis=0, keepdims=True), axis=1, keepdims=True)


def share_and_build_kernel(
    observations_hbm, gains_hbm, observed_hbm, pattern_hbm, transition_hbm,
    y_hbm, s_hi_hbm, s_lo_hbm, packed_hbm,
    y_ref, s_hi, s_lo,
    observations_ref, gains_ref, observed_ref, pattern_ref, transition_ref,
    own, slots, n_hi, x_ref, load_sem, save_sem, send_sem, recv_sem,
):
    loads = []
    for place, (source, target) in enumerate((
        (observations_hbm, observations_ref),
        (gains_hbm, gains_ref),
        (observed_hbm, observed_ref),
        (pattern_hbm, pattern_ref),
        (transition_hbm, transition_ref),
    )):
        loads.append(pltpu.make_async_copy(source, target, load_sem.at[place]))
        loads[-1].start()
    size = transition_ref.shape[0]
    blocks = pattern_ref.shape[0]
    block = size // blocks
    frames = observations_ref.shape[0]
    count = slots.shape[0]
    mine = lax.axis_index("tm")
    eye = functools.partial(eye_of, size)

    chips = count // 2
    core = lax.rem(mine, 2)
    chip = mine // 2
    partner = {"tm": 2 * chip + 1 - core}
    others = [2 * lax.rem(chip + hop, chips) + core for hop in range(1, chips)]
    sources = [2 * lax.rem(chip + chips - hop, chips) + core for hop in range(1, chips)]

    barrier = pltpu.get_barrier_semaphore()
    for target in [partner] + [{"tm": other} for other in others]:
        pl.semaphore_signal(barrier, inc=1, device_id=target, device_id_type=MESH)
    for load in loads[:3]:
        load.wait()
    seen = gains_ref[...] * observed_ref[...].astype(F32)
    own[:, :size] = 1.0 - seen
    own[:, size:] = seen * observations_ref[...]
    pl.semaphore_wait(barrier, chips)

    def send(source, place, target, sem):
        copy = pltpu.make_async_remote_copy(
            src_ref=source,
            dst_ref=slots.at[place],
            send_sem=send_sem.at[sem],
            recv_sem=recv_sem.at[sem],
            device_id=target,
            device_id_type=MESH,
        )
        copy.start()
        return copy

    direct = [
        send(own, mine, {"tm": other}, hop) for hop, other in enumerate(others, 1)
    ]
    passed = [send(own, mine, partner, 0)]

    for load in loads[3:]:
        load.wait()
    tall = (
        lax.broadcasted_iota(jnp.int32, (size, blocks), 0) // block
        == lax.broadcasted_iota(jnp.int32, (size, blocks), 1)
    ).astype(BF16)
    wide = (
        lax.broadcasted_iota(jnp.int32, (blocks, size), 1) // block
        == lax.broadcasted_iota(jnp.int32, (blocks, size), 0)
    ).astype(BF16)
    present = jnp.maximum(pattern_ref[...].astype(F32), eye_of(blocks)).astype(BF16)
    expand = dot1(dot1(tall, present).astype(BF16), wide)
    masked = transition_ref[...] * expand
    skew = 0.5 * (masked.T - masked)
    high, low = split(skew)
    s_hi[...] = high
    s_lo[...] = low
    saves = [
        pltpu.make_async_copy(s_hi, s_hi_hbm, save_sem.at[0]),
        pltpu.make_async_copy(s_lo, s_lo_hbm, save_sem.at[1]),
    ]
    for save in saves:
        save.start()

    normal = eye() - dot1(high, high)
    n_hi[...] = normal.astype(BF16)
    square = dot1(n_hi[...], n_hi[...])
    bound = 1.02 * jnp.sqrt(jnp.sqrt(0.5 * total(square * square)))
    bound = jnp.maximum(bound, 1.0001)

    def rescale(rho):
        worst = jnp.minimum(rho * rho, 1.0)
        return 2.0 / (2.0 - worst), worst / (2.0 - worst)

    alpha = 2.0 / (1.0 + bound)
    factor, rho = rescale((bound - 1.0) / (bound + 1.0))
    x_ref[...] = (factor * alpha) * (2.0 * eye() - alpha * normal)

    def newton(step, rho):
        x_hi = x_ref[...].astype(BF16)
        res = eye() - dot1(n_hi[...], x_hi)
        factor, rho = rescale(rho)
        x_ref[...] = factor * (x_ref[...] + dot1(x_hi, res.astype(BF16)))
        return rho

    rho = lax.fori_loop(0, NEWTON_STEPS - 1, newton, rho)
    for hop, source in enumerate(sources, 1):
        direct[hop - 1].wait_recv()
        passed.append(send(slots.at[source], source, partner, chips + hop))
    newton(0, rho)
    y_ref[...] = x_ref[...] + dot1(x_ref[...].astype(BF16), s_hi[...])

    saves.append(pltpu.make_async_copy(y_ref, y_hbm, save_sem.at[2]))
    saves[-1].start()
    for copy in passed:
        copy.wait_recv()
    slots[mine] = own[...]
    saves.append(pltpu.make_async_copy(slots, packed_hbm, save_sem.at[3]))
    saves[-1].start()
    for save in saves:
        save.wait()
    for copy in direct + passed:
        copy.wait_send()


def share_and_build(observations, gains, observed, pattern, transition):
    frames, size = observations.shape
    count = lax.axis_size("tm")
    square = (size, size)
    return pl.pallas_call(
        share_and_build_kernel,
        out_shape=(
            jax.ShapeDtypeStruct(square, F32),
            jax.ShapeDtypeStruct(square, BF16),
            jax.ShapeDtypeStruct(square, BF16),
            jax.ShapeDtypeStruct((count, frames, 2 * size), F32),
        ),
        in_specs=[HBM] * 5,
        out_specs=(HBM,) * 4,
        scratch_shapes=[
            pltpu.VMEM(square, F32),
            pltpu.VMEM(square, BF16),
            pltpu.VMEM(square, BF16),
            pltpu.VMEM((frames, size), F32),
            pltpu.VMEM((frames, size), F32),
            pltpu.VMEM((frames, size), jnp.int32),
            pltpu.VMEM(pattern.shape, jnp.int32),
            pltpu.VMEM(square, F32),
            pltpu.VMEM((frames, 2 * size), F32),
            pltpu.VMEM((count, frames, 2 * size), F32),
            pltpu.VMEM(square, BF16),
            pltpu.VMEM(square, F32),
            pltpu.SemaphoreType.DMA((5,)),
            pltpu.SemaphoreType.DMA((4,)),
            pltpu.SemaphoreType.DMA((count,)),
            pltpu.SemaphoreType.DMA((count,)),
        ],
        compiler_params=pltpu.CompilerParams(
            vmem_limit_bytes=60 << 20, collective_id=0, has_side_effects=True
        ),
        name="share_and_build",
    )(observations, gains, observed, pattern, transition)


def refine_to_transition(s_hi, s_lo, ft_ref, r_ref, y_hi, y_lo):
    size = ft_ref.shape[0]
    eye = functools.partial(eye_of, size)

    def residual():
        high, low = split(ft_ref[...])
        y_hi[...] = high
        y_lo[...] = low
        prod = dot1(s_hi[...], y_lo[...]) + dot1(s_lo[...], y_hi[...])
        res = eye() - ft_ref[...] + (prod + dot1(s_hi[...], y_hi[...]))
        r_ref[...] = res
        return jnp.max(total(res * res))

    first = residual()
    good = first < 0.5

    @pl.when(jnp.logical_not(good))
    def _():
        skew = s_hi[...].astype(F32) + s_lo[...].astype(F32)
        ft_ref[...] = (1.9 / (2.0 + total(skew * skew))) * (eye() + skew)
        residual()

    def unfinished(carry):
        step, size2 = carry
        return jnp.logical_and(jnp.logical_not(size2 < 6e-5), step < 64)

    def refine(carry):
        step, unused = carry
        r_hi, r_lo = split(r_ref[...])
        ft_ref[...] += dot1(y_hi[...], r_hi)

        @pl.when(step > 0)
        def _():
            ft_ref[...] += dot1(y_hi[...], r_lo) + dot1(y_lo[...], r_hi)

        return step + 1, residual()

    lax.while_loop(
        unfinished, refine, (jnp.where(good, 0, 1), jnp.where(good, first, 1e9))
    )
    last = ft_ref[...] + dot1(y_hi[...], r_ref[...].astype(BF16))
    ft_ref[...] = 2.0 * last - eye()


def scan_kernel(
    y_hbm, s_hi_hbm, s_lo_hbm, frames_hbm, start_hbm, out_ref,
    ft_ref, s_hi, s_lo, frames_ref, start_ref, r_ref, y_hi, y_lo, kept,
    f_ref, moved_drive, damp_parts, columns, load_sem,
):
    loads = []
    for place, (source, target) in enumerate((
        (y_hbm, ft_ref),
        (s_hi_hbm, s_hi),
        (s_lo_hbm, s_lo),
        (frames_hbm, frames_ref),
        (start_hbm, start_ref),
    )):
        loads.append(pltpu.make_async_copy(source, target, load_sem.at[place]))
        loads[-1].start()
    for load in loads[:3]:
        load.wait()
    refine_to_transition(s_hi, s_lo, ft_ref, r_ref, y_hi, y_lo)
    for load in loads[3:]:
        load.wait()
    size = ft_ref.shape[0]
    frames, width = out_ref.shape
    tiles = size // 128
    groups = size // 8
    mine = lax.axis_index("tm")
    offset = 0 if width == size else lax.axis_index("state") * width
    f_ref[...] = ft_ref[...].T

    ft_hi, ft_lo = split(ft_ref[...])
    drive_hi, drive_lo = split(frames_ref[:, size:])
    moved_drive[...] = (dot1(drive_hi, ft_lo) + dot1(drive_lo, ft_hi)) + dot1(drive_hi, ft_hi)

    def finish(acc, t, extra):
        moved = jnp.sum(acc[0] + acc[1], axis=0, keepdims=True) + extra
        return frames_ref[pl.ds(t, 1), :size] * moved + frames_ref[pl.ds(t, 1), size:]

    def earlier_chunk(chunk, row):
        base = pl.multiple_of(chunk * frames, frames)
        damp = frames_ref[pl.ds(base, frames), :size].T
        high, low = split(damp)
        least = (damp - high.astype(F32) - low.astype(F32)).astype(BF16)
        for place, part in enumerate((high, low, least)):
            damp_parts[:, frames * place : frames * (place + 1)] = part
        at = lax.broadcasted_iota(jnp.int32, (3 * frames, 256), 0)
        lane = lax.broadcasted_iota(jnp.int32, (3 * frames, 256), 1)

        def spread_damp(four):
            wanted = 4 * four + 2 * (lane // 128)
            pick = (lax.rem(at, frames) == wanted).astype(BF16)
            return dot1(damp_parts[...], pick)

        def pair(t, row, now, half):
            spread = jnp.broadcast_to(row, (8, size))
            acc = [jnp.zeros((8, size), F32), jnp.zeros((8, size), F32)]
            for group in range(groups):
                rows = slice(8 * group, 8 * group + 8)
                part = f_ref[rows, :] * spread
                part = sum(part[:, 128 * k : 128 * k + 128] for k in range(tiles))
                column = jnp.broadcast_to(jnp.sum(part, axis=1, keepdims=True), (8, 128))
                column = column * columns[now, rows, 128 * half : 128 * half + 128]
                acc[group % 2] += ft_ref[rows, :] * jnp.concatenate([column] * tiles, 1)
            return finish(acc, t + 1, moved_drive[pl.ds(t, 1), :])

        def fours(four, row):
            now = lax.rem(four, 2)
            row = pair(base + 4 * four, row, now, 0)
            columns[1 - now] = spread_damp(four + 1)
            return pair(base + 4 * four + 2, row, now, 1)

        columns[0] = spread_damp(0)
        return lax.fori_loop(0, frames // 4, fours, row)

    row = lax.fori_loop(0, mine, earlier_chunk, start_ref[...])

    def step(local, row):
        acc = [jnp.zeros((8, size), F32), jnp.zeros((8, size), F32)]
        for tile in range(tiles):
            piece = row[:, 128 * tile : 128 * tile + 128]
            column = jnp.broadcast_to(piece, (128, 128)).T
            for group in range(16):
                at = 128 * tile + 8 * group
                spread = jnp.concatenate([column[8 * group : 8 * group + 8]] * tiles, 1)
                acc[group % 2] += ft_ref[at : at + 8, :] * spread
        row = finish(acc, mine * frames + local, 0.0)
        kept[pl.ds(local, 1), :] = row
        return row

    lax.fori_loop(0, frames, step, row)
    if width == size:
        out_ref[...] = kept[...]
    else:
        out_ref[...] = kept[:, pl.ds(pl.multiple_of(offset, width), width)]


def body(observations, gains, observed, pattern, transition, initial_mean):
    frames, size = observations.shape
    width = size // lax.axis_size("state")
    start, s_hi, s_lo, packed = share_and_build(
        observations, gains, observed, pattern, transition
    )
    packed = packed.reshape(-1, 2 * size)
    kept_width = width if width % 128 == 0 else size
    square = (size, size)
    means = pl.pallas_call(
        scan_kernel,
        out_shape=jax.ShapeDtypeStruct((frames, kept_width), F32),
        in_specs=[HBM] * 5,
        out_specs=VMEM,
        scratch_shapes=[
            pltpu.VMEM(square, F32),
            pltpu.VMEM(square, BF16),
            pltpu.VMEM(square, BF16),
            pltpu.VMEM((packed.shape[0], 2 * size), F32),
            pltpu.VMEM((1, size), F32),
            pltpu.VMEM(square, F32),
            pltpu.VMEM(square, BF16),
            pltpu.VMEM(square, BF16),
            pltpu.VMEM((frames, size), F32),
            pltpu.VMEM(square, F32),
            pltpu.VMEM((packed.shape[0], size), F32),
            pltpu.VMEM((size, 3 * frames), BF16),
            pltpu.VMEM((2, size, 256), F32),
            pltpu.SemaphoreType.DMA((5,)),
        ],
        compiler_params=pltpu.CompilerParams(vmem_limit_bytes=60 << 20),
        name="refine_and_scan",
    )(start, s_hi, s_lo, packed, initial_mean.reshape(1, size))
    if kept_width == width:
        return means
    return lax.dynamic_slice_in_dim(means, lax.axis_index("state") * width, width, 1)


def solution(mesh):
    return jax.shard_map(
        body,
        mesh=mesh,
        in_specs=(
            P(("seg", "tm"), None),
            P(("seg", "tm"), None),
            P(("seg", "tm"), None),
            P(),
            P(),
            P("seg"),
        ),
        out_specs=P(("seg", "tm"), "state"),
        check_vma=False,
    )
```

```python
import functools

import jax
import jax.numpy as jnp
from jax import lax
from jax.experimental import pallas as pl
from jax.experimental.pallas import tpu as pltpu
from jax.sharding import PartitionSpec as P

F32 = jnp.float32
BF16 = jnp.bfloat16
VMEM = pl.BlockSpec(memory_space=pltpu.VMEM)
HBM = pl.BlockSpec(memory_space=pltpu.HBM)
MESH = pl.DeviceIdType.MESH
NEWTON_STEPS = 3


def split(a):
    high = a.astype(BF16)
    return high, (a - high.astype(F32)).astype(BF16)


def dot1(a, b):
    return jnp.dot(a, b, preferred_element_type=F32)


def eye_of(size):
    rows = lax.broadcasted_iota(jnp.int32, (size, size), 0)
    cols = lax.broadcasted_iota(jnp.int32, (size, size), 1)
    return (rows == cols).astype(F32)


def total(a):
    return jnp.sum(jnp.sum(a, axis=0, keepdims=True), axis=1, keepdims=True)


def share_and_build_kernel(
    observations_hbm, gains_hbm, observed_hbm, pattern_hbm, transition_hbm,
    y_hbm, s_hi_hbm, s_lo_hbm, packed_hbm,
    y_ref, s_hi, s_lo,
    observations_ref, gains_ref, observed_ref, pattern_ref, transition_ref,
    own, slots, n_hi, x_ref, load_sem, save_sem, send_sem, recv_sem,
):
    loads = []
    for place, (source, target) in enumerate((
        (observations_hbm, observations_ref),
        (gains_hbm, gains_ref),
        (observed_hbm, observed_ref),
        (pattern_hbm, pattern_ref),
        (transition_hbm, transition_ref),
    )):
        loads.append(pltpu.make_async_copy(source, target, load_sem.at[place]))
        loads[-1].start()
    size = transition_ref.shape[0]
    blocks = pattern_ref.shape[0]
    block = size // blocks
    frames = observations_ref.shape[0]
    count = slots.shape[0]
    mine = lax.axis_index("tm")
    eye = functools.partial(eye_of, size)

    chips = count // 2
    core = lax.rem(mine, 2)
    chip = mine // 2
    partner = {"tm": 2 * chip + 1 - core}
    others = [2 * lax.rem(chip + hop, chips) + core for hop in range(1, chips)]
    sources = [2 * lax.rem(chip + chips - hop, chips) + core for hop in range(1, chips)]

    barrier = pltpu.get_barrier_semaphore()
    for target in [partner] + [{"tm": other} for other in others]:
        pl.semaphore_signal(barrier, inc=1, device_id=target, device_id_type=MESH)
    for load in loads[:3]:
        load.wait()
    seen = gains_ref[...] * observed_ref[...].astype(F32)
    own[:, :size] = 1.0 - seen
    own[:, size:] = seen * observations_ref[...]
    pl.semaphore_wait(barrier, chips)

    def send(source, place, target, sem):
        copy = pltpu.make_async_remote_copy(
            src_ref=source,
            dst_ref=slots.at[place],
            send_sem=send_sem.at[sem],
            recv_sem=recv_sem.at[sem],
            device_id=target,
            device_id_type=MESH,
        )
        copy.start()
        return copy

    direct = [
        send(own, mine, {"tm": other}, hop) for hop, other in enumerate(others, 1)
    ]
    passed = [send(own, mine, partner, 0)]

    for load in loads[3:]:
        load.wait()
    tall = (
        lax.broadcasted_iota(jnp.int32, (size, blocks), 0) // block
        == lax.broadcasted_iota(jnp.int32, (size, blocks), 1)
    ).astype(BF16)
    wide = (
        lax.broadcasted_iota(jnp.int32, (blocks, size), 1) // block
        == lax.broadcasted_iota(jnp.int32, (blocks, size), 0)
    ).astype(BF16)
    present = jnp.maximum(pattern_ref[...].astype(F32), eye_of(blocks)).astype(BF16)
    expand = dot1(dot1(tall, present).astype(BF16), wide)
    masked = transition_ref[...] * expand
    skew = 0.5 * (masked.T - masked)
    high, low = split(skew)
    s_hi[...] = high
    s_lo[...] = low
    saves = [
        pltpu.make_async_copy(s_hi, s_hi_hbm, save_sem.at[0]),
        pltpu.make_async_copy(s_lo, s_lo_hbm, save_sem.at[1]),
    ]
    for save in saves:
        save.start()

    normal = eye() - dot1(high, high)
    n_hi[...] = normal.astype(BF16)
    square = dot1(n_hi[...], n_hi[...])
    bound = 1.02 * jnp.sqrt(jnp.sqrt(0.5 * total(square * square)))
    bound = jnp.maximum(bound, 1.0001)

    def rescale(rho):
        worst = jnp.minimum(rho * rho, 1.0)
        return 2.0 / (2.0 - worst), worst / (2.0 - worst)

    alpha = 2.0 / (1.0 + bound)
    factor, rho = rescale((bound - 1.0) / (bound + 1.0))
    x_ref[...] = (factor * alpha) * (2.0 * eye() - alpha * normal)

    def newton(step, rho):
        x_hi = x_ref[...].astype(BF16)
        res = eye() - dot1(n_hi[...], x_hi)
        factor, rho = rescale(rho)
        x_ref[...] = factor * (x_ref[...] + dot1(x_hi, res.astype(BF16)))
        return rho

    rho = lax.fori_loop(0, NEWTON_STEPS - 1, newton, rho)
    for hop, source in enumerate(sources, 1):
        direct[hop - 1].wait_recv()
        passed.append(send(slots.at[source], source, partner, chips + hop))
    newton(0, rho)
    y_ref[...] = x_ref[...] + dot1(x_ref[...].astype(BF16), s_hi[...])

    saves.append(pltpu.make_async_copy(y_ref, y_hbm, save_sem.at[2]))
    saves[-1].start()
    for copy in passed:
        copy.wait_recv()
    slots[mine] = own[...]
    saves.append(pltpu.make_async_copy(slots, packed_hbm, save_sem.at[3]))
    saves[-1].start()
    for save in saves:
        save.wait()
    for copy in direct + passed:
        copy.wait_send()


def share_and_build(observations, gains, observed, pattern, transition):
    frames, size = observations.shape
    count = lax.axis_size("tm")
    square = (size, size)
    return pl.pallas_call(
        share_and_build_kernel,
        out_shape=(
            jax.ShapeDtypeStruct(square, F32),
            jax.ShapeDtypeStruct(square, BF16),
            jax.ShapeDtypeStruct(square, BF16),
            jax.ShapeDtypeStruct((count, frames, 2 * size), F32),
        ),
        in_specs=[HBM] * 5,
        out_specs=(HBM,) * 4,
        scratch_shapes=[
            pltpu.VMEM(square, F32),
            pltpu.VMEM(square, BF16),
            pltpu.VMEM(square, BF16),
            pltpu.VMEM((frames, size), F32),
            pltpu.VMEM((frames, size), F32),
            pltpu.VMEM((frames, size), jnp.int32),
            pltpu.VMEM(pattern.shape, jnp.int32),
            pltpu.VMEM(square, F32),
            pltpu.VMEM((frames, 2 * size), F32),
            pltpu.VMEM((count, frames, 2 * size), F32),
            pltpu.VMEM(square, BF16),
            pltpu.VMEM(square, F32),
            pltpu.SemaphoreType.DMA((5,)),
            pltpu.SemaphoreType.DMA((4,)),
            pltpu.SemaphoreType.DMA((count,)),
            pltpu.SemaphoreType.DMA((count,)),
        ],
        compiler_params=pltpu.CompilerParams(
            vmem_limit_bytes=60 << 20, collective_id=0, has_side_effects=True
        ),
        name="share_and_build",
    )(observations, gains, observed, pattern, transition)


def refine_to_transition(s_hi, s_lo, ft_ref, r_ref, y_hi, y_lo):
    size = ft_ref.shape[0]
    eye = functools.partial(eye_of, size)

    def residual():
        high, low = split(ft_ref[...])
        y_hi[...] = high
        y_lo[...] = low
        prod = dot1(s_hi[...], y_lo[...]) + dot1(s_lo[...], y_hi[...])
        res = eye() - ft_ref[...] + (prod + dot1(s_hi[...], y_hi[...]))
        r_ref[...] = res
        return jnp.max(total(res * res))

    first = residual()
    good = first < 0.5

    @pl.when(jnp.logical_not(good))
    def _():
        skew = s_hi[...].astype(F32) + s_lo[...].astype(F32)
        ft_ref[...] = (1.9 / (2.0 + total(skew * skew))) * (eye() + skew)
        residual()

    def unfinished(carry):
        step, size2 = carry
        return jnp.logical_and(jnp.logical_not(size2 < 6e-5), step < 64)

    def refine(carry):
        step, unused = carry
        r_hi, r_lo = split(r_ref[...])
        ft_ref[...] += dot1(y_hi[...], r_hi)

        @pl.when(step > 0)
        def _():
            ft_ref[...] += dot1(y_hi[...], r_lo) + dot1(y_lo[...], r_hi)

        return step + 1, residual()

    lax.while_loop(
        unfinished, refine, (jnp.where(good, 0, 1), jnp.where(good, first, 1e9))
    )
    last = ft_ref[...] + dot1(y_hi[...], r_ref[...].astype(BF16))
    ft_ref[...] = 2.0 * last - eye()


def scan_kernel(
    y_hbm, s_hi_hbm, s_lo_hbm, frames_hbm, start_hbm, out_ref,
    ft_ref, s_hi, s_lo, frames_ref, start_ref, r_ref, y_hi, y_lo, kept,
    f_ref, moved_drive, before, damp_parts, columns, load_sem,
):
    loads = []
    for place, (source, target) in enumerate((
        (y_hbm, ft_ref),
        (s_hi_hbm, s_hi),
        (s_lo_hbm, s_lo),
        (frames_hbm, frames_ref),
        (start_hbm, start_ref),
    )):
        loads.append(pltpu.make_async_copy(source, target, load_sem.at[place]))
        loads[-1].start()
    for load in loads[:3]:
        load.wait()
    refine_to_transition(s_hi, s_lo, ft_ref, r_ref, y_hi, y_lo)
    for load in loads[3:]:
        load.wait()
    size = ft_ref.shape[0]
    frames, width = out_ref.shape
    tiles = size // 128
    groups = size // 8
    mine = lax.axis_index("tm")
    offset = 0 if width == size else lax.axis_index("state") * width
    f_ref[...] = ft_ref[...].T

    ft_hi, ft_lo = split(ft_ref[...])
    drive_hi, drive_lo = split(frames_ref[:, size:])
    moved_drive[...] = (dot1(drive_hi, ft_lo) + dot1(drive_lo, ft_hi)) + dot1(drive_hi, ft_hi)

    def finish(acc, t, extra):
        moved = jnp.sum(acc[0] + acc[1], axis=0, keepdims=True) + extra
        return frames_ref[pl.ds(t, 1), :size] * moved + frames_ref[pl.ds(t, 1), size:]

    def one_chunk(chunk, row):
        base = pl.multiple_of(chunk * frames, frames)
        damp = frames_ref[pl.ds(base, frames), :size].T
        high, low = split(damp)
        least = (damp - high.astype(F32) - low.astype(F32)).astype(BF16)
        for place, part in enumerate((high, low, least)):
            damp_parts[:, frames * place : frames * (place + 1)] = part
        at = lax.broadcasted_iota(jnp.int32, (3 * frames, 256), 0)
        lane = lax.broadcasted_iota(jnp.int32, (3 * frames, 256), 1)

        def spread_damp(four):
            wanted = 4 * four + 2 * (lane // 128)
            pick = (lax.rem(at, frames) == wanted).astype(BF16)
            return dot1(damp_parts[...], pick)

        def pair(t, row, now, half):
            before[pl.ds((t - base) // 2, 1), :] = row
            spread = jnp.broadcast_to(row, (8, size))
            acc = [jnp.zeros((8, size), F32), jnp.zeros((8, size), F32)]
            for group in range(groups):
                rows = slice(8 * group, 8 * group + 8)
                part = f_ref[rows, :] * spread
                part = sum(part[:, 128 * k : 128 * k + 128] for k in range(tiles))
                column = jnp.broadcast_to(jnp.sum(part, axis=1, keepdims=True), (8, 128))
                column = column * columns[now, rows, 128 * half : 128 * half + 128]
                acc[group % 2] += ft_ref[rows, :] * jnp.concatenate([column] * tiles, 1)
            row = finish(acc, t + 1, moved_drive[pl.ds(t, 1), :])
            kept[pl.ds(t - base + 1, 1), :] = row
            return row

        def fours(four, row):
            now = lax.rem(four, 2)
            row = pair(base + 4 * four, row, now, 0)
            columns[1 - now] = spread_damp(four + 1)
            return pair(base + 4 * four + 2, row, now, 1)

        columns[0] = spread_damp(0)
        return lax.fori_loop(0, frames // 4, fours, row)

    lax.fori_loop(0, mine + 1, one_chunk, start_ref[...])

    high, low = split(before[...])
    before[...] = (dot1(high, ft_lo) + dot1(low, ft_hi)) + dot1(high, ft_hi)
    for place in range(frames // 2):
        at = mine * frames + 2 * place
        kept[2 * place : 2 * place + 1, :] = (
            frames_ref[pl.ds(at, 1), :size] * before[place : place + 1, :]
            + frames_ref[pl.ds(at, 1), size:]
        )
    if width == size:
        out_ref[...] = kept[...]
    else:
        out_ref[...] = kept[:, pl.ds(pl.multiple_of(offset, width), width)]


def body(observations, gains, observed, pattern, transition, initial_mean):
    frames, size = observations.shape
    width = size // lax.axis_size("state")
    start, s_hi, s_lo, packed = share_and_build(
        observations, gains, observed, pattern, transition
    )
    packed = packed.reshape(-1, 2 * size)
    kept_width = width if width % 128 == 0 else size
    square = (size, size)
    means = pl.pallas_call(
        scan_kernel,
        out_shape=jax.ShapeDtypeStruct((frames, kept_width), F32),
        in_specs=[HBM] * 5,
        out_specs=VMEM,
        scratch_shapes=[
            pltpu.VMEM(square, F32),
            pltpu.VMEM(square, BF16),
            pltpu.VMEM(square, BF16),
            pltpu.VMEM((packed.shape[0], 2 * size), F32),
            pltpu.VMEM((1, size), F32),
            pltpu.VMEM(square, F32),
            pltpu.VMEM(square, BF16),
            pltpu.VMEM(square, BF16),
            pltpu.VMEM((frames, size), F32),
            pltpu.VMEM(square, F32),
            pltpu.VMEM((packed.shape[0], size), F32),
            pltpu.VMEM((frames // 2, size), F32),
            pltpu.VMEM((size, 3 * frames), BF16),
            pltpu.VMEM((2, size, 256), F32),
            pltpu.SemaphoreType.DMA((5,)),
        ],
        compiler_params=pltpu.CompilerParams(vmem_limit_bytes=60 << 20),
        name="refine_and_scan",
    )(start, s_hi, s_lo, packed, initial_mean.reshape(1, size))
    if kept_width == width:
        return means
    return lax.dynamic_slice_in_dim(means, lax.axis_index("state") * width, width, 1)


def solution(mesh):
    return jax.shard_map(
        body,
        mesh=mesh,
        in_specs=(
            P(("seg", "tm"), None),
            P(("seg", "tm"), None),
            P(("seg", "tm"), None),
            P(),
            P(),
            P("seg"),
        ),
        out_specs=P(("seg", "tm"), "state"),
        check_vma=False,
    )
```
